32 devices in a mesh: view: 4 (over y, x), tile: 8 (over z, core).
Axes of the slice: x: 2, y: 2, z: 4, core: 2. Of those that a mesh axis runs over, the one named last changes fastest.
Arguments:
- estimate: float32 [64, 256, 128], P('tile', 'view'), may hold values from 0.5 to 1.5
- images: float32 [4, 64, 256, 128], P('view', 'tile'), may hold values from 0.25 to 4
- taps_first: float32 [4, 5], P('view'), may hold values from 0.1 to 1
- taps_second: float32 [4, 7], P('view'), may hold values from 0.1 to 1
- taps_axial: float32 [4, 33], P('view'), may hold values from 0.02 to 0.2
Outputs:
- deconvolved: float32 [64, 256, 128], P('tile', 'view')
The draws below stay inside these ranges and needn't reach their ends.
All inputs are finite; a program needn't handle non-finite values.
Results may differ from the reference program's by a relative error of at most 0.0001.
Values sent between devices are 32-bit elements; how exact they have to be, the bound alone decides.
A program may use at most 64 MiB of HBM per device.

```python
import math
import jax
import jax.numpy as jnp
from jax import lax

NY = 256
NZ = 128
RX = 2
RY = 3
RZ = 16
ITERS = 2
VIEWS = 4
NX = 64


def level_of(rng, dims, split, smallest, largest):
    gain = 1.0
    for dim, shards_of in split:
        draws = jax.random.uniform(jax.random.fold_in(jax.random.fold_in(rng, 6), dim), (shards_of,), jnp.float32, smallest / len(split), largest / len(split))
        gain = gain * jnp.repeat(jnp.exp(draws), dims[dim] // shards_of).reshape((-1,) + (1,) * (len(dims) - 1 - dim))
    return gain


def setup_inputs(seed: int = 0) -> dict:
    streams_of = jax.random.split(jax.random.key(seed), 6)
    return {
        "estimate": jnp.clip(0.5 + 1.0 * jax.random.uniform(streams_of[0], (NX, NY, NZ), jnp.float32) ** level_of(streams_of[0], (NX, NY, NZ), ((0, 8), (1, 4)), -0.2, 0.2), 0.5, 1.5),
        "images": jnp.clip(jnp.exp(math.log(4.0) - 2.7725887 * jax.random.uniform(streams_of[1], (VIEWS, NX, NY, NZ), jnp.float32) ** level_of(streams_of[1], (VIEWS, NX, NY, NZ), ((0, 4), (1, 8)), -0.2, 0.2)), 0.25, 4.0),
        "taps_first": jnp.clip(jnp.exp(math.log(1.0) - 2.3025851 * jax.random.uniform(streams_of[2], (VIEWS, 2 * RX + 1), jnp.float32) ** level_of(streams_of[2], (VIEWS, 2 * RX + 1), ((0, 4),), -0.2, 0.2)), 0.1, 1.0),
        "taps_second": jnp.clip(jnp.exp(math.log(1.0) - 2.3025851 * jax.random.uniform(streams_of[3], (VIEWS, 2 * RY + 1), jnp.float32) ** level_of(streams_of[3], (VIEWS, 2 * RY + 1), ((0, 4),), -0.2, 0.2)), 0.1, 1.0),
        "taps_axial": jnp.clip(jnp.exp(math.log(0.2) - 2.3025851 * jax.random.uniform(streams_of[4], (VIEWS, 2 * RZ + 1), jnp.float32) ** level_of(streams_of[4], (VIEWS, 2 * RZ + 1), ((0, 4),), -0.2, 0.2)), 0.02, 0.2),
    }


def toeplitz(taps, length, radius):
    index = jnp.arange(length, dtype=jnp.int32)
    offset = index[None, :] - index[:, None] + radius
    count = taps.shape[0]
    onehot = (offset[None, :, :] == jnp.arange(count, dtype=jnp.int32)[:, None, None]).astype(jnp.float32)
    return jnp.sum(onehot * taps[:, None, None], axis=0)


def along_axial(field, matrix):
    flat = field.reshape(-1, field.shape[2])
    out = jnp.dot(flat, matrix, precision=lax.Precision.HIGHEST, preferred_element_type=jnp.float32)
    return out.reshape(field.shape)


def along_second(field, taps, reverse):
    count = taps.shape[0]
    radius = (count - 1) // 2
    length = field.shape[1]
    padded = jnp.pad(field, ((0, 0), (radius, radius), (0, 0)))
    total = jnp.zeros(field.shape, jnp.float32)
    for tap in range(count):
        start = tap if reverse else 2 * radius - tap
        total = total + taps[tap] * padded[:, start:start + length, :]
    return total


def along_first(padded, taps, reverse):
    count = taps.shape[0]
    radius = (count - 1) // 2
    length = padded.shape[0] - 2 * radius
    total = jnp.zeros((length,) + padded.shape[1:], jnp.float32)
    for tap in range(count):
        start = tap if reverse else 2 * radius - tap
        total = total + taps[tap] * padded[start:start + length]
    return total


def pad_first(field, radius):
    return jnp.pad(field, ((radius, radius), (0, 0), (0, 0)))


def one_view(current, image, first, second, axial):
    radius = (first.shape[0] - 1) // 2
    matrix = toeplitz(axial, current.shape[2], (axial.shape[0] - 1) // 2)
    inner = along_second(along_axial(current, matrix), second, False)
    blurred = along_first(pad_first(inner, radius), first, False)
    ratio = image / blurred
    inner = along_second(along_axial(ratio, matrix.T), second, True)
    return along_first(pad_first(inner, radius), first, True)


def reference(estimate, images, taps_first, taps_second, taps_axial):
    current = estimate
    for step in range(ITERS):
        def accumulate(carry, items):
            return carry + one_view(current, items[0], items[1], items[2], items[3]), None

        total, unused = lax.scan(accumulate, jnp.zeros(current.shape, jnp.float32), (images, taps_first, taps_second, taps_axial))
        current = current * (total / VIEWS)
    return current
```

```python
import functools

import jax
import jax.numpy as jnp
from jax import lax
from jax.experimental import pallas as pl
from jax.experimental.pallas import tpu as pltpu
from jax.sharding import PartitionSpec as P

ITERS = 2
PAD = 8
DIRECTIONS = [(0, -1), (0, 1), (-1, -1), (-1, 1), (1, -1), (1, 1), (-1, 0), (1, 0)]
MESH_ID = pl.DeviceIdType.MESH


def split(x):
    hi = x.astype(jnp.bfloat16)
    lo = (x - hi.astype(jnp.float32)).astype(jnp.bfloat16)
    return hi, lo


def kernel(
    views, tiles, rf, rs, ra,
    est_ref, img_ref, tf_ref, ts_ref, ta_ref, out_ref,
    est, ext, planes, bplane, rplane, gplanes, left, left2, wconv, wcorr, pack, img, over,
    img_send, img_recv, pk_send, pk_recv, local_sem, h_send, h_recv, o_send, o_recv,
):
    nx, ny, nz = est_ref.shape
    nf, ns, na = 2 * rf + 1, 2 * rs + 1, 2 * ra + 1
    frame = ny + 2 * PAD
    full = nx + 2 * rf
    v = lax.axis_index("view")
    t = lax.axis_index("tile")
    mid = pl.ds(PAD, ny)
    f32 = jnp.float32

    def inside(dt, dv):
        ok = None
        for d, at, count in ((dt, t, tiles), (dv, v, views)):
            if d:
                here = at + d < count if d > 0 else at + d >= 0
                ok = here if ok is None else jnp.logical_and(ok, here)
        return ok

    own = pltpu.make_async_copy(
        img_ref.at[0, :, pl.ds(pl.multiple_of(v * ny, 8), ny), :], img.at[v], local_sem
    )
    own.start()

    for it in range(ITERS):
        est[it] = jnp.zeros(est.shape[1:], f32)
    est[0, rf : rf + nx, mid, :] = est_ref[...]
    pack[v] = jnp.zeros(pack.shape[1:], f32)
    for k in range(nf):
        pack[v, k : k + 1, :] = jnp.broadcast_to(tf_ref[0:1, k : k + 1], (1, nz))
    for k in range(ns):
        pack[v, nf + k : nf + k + 1, :] = jnp.broadcast_to(ts_ref[0:1, k : k + 1], (1, nz))
    pack[v, nf + ns : nf + ns + 1, 0:na] = ta_ref[...]

    barrier = pltpu.get_barrier_semaphore()
    for d in range(1, views):
        peer = lax.rem(v + d, views)
        pl.semaphore_signal(barrier, inc=1, device_id=(peer, t), device_id_type=MESH_ID)
    for dt, dv in DIRECTIONS:
        if dt:
            @pl.when(inside(dt, dv))
            def _(dt=dt, dv=dv):
                pl.semaphore_signal(
                    barrier, inc=1, device_id=(v + dv, t + dt), device_id_type=MESH_ID
                )
    sides = jnp.where(t > 0, 1, 0) + jnp.where(t < tiles - 1, 1, 0)
    rows = 1 + jnp.where(v > 0, 1, 0) + jnp.where(v < views - 1, 1, 0)
    pl.semaphore_wait(barrier, views - 1 + sides * rows)

    def halo(it, n):
        dt, dv = DIRECTIONS[n]
        sp, dp, cp = {0: (rf, rf, nx), 1: (nx, 0, rf), -1: (rf, rf + nx, rf)}[dt]
        sr, dr, cr = {0: (PAD, PAD, ny), 1: (ny, 0, PAD), -1: (PAD, PAD + ny, PAD)}[dv]
        return pltpu.make_async_remote_copy(
            src_ref=est.at[it, pl.ds(sp, cp), pl.ds(sr, cr), :],
            dst_ref=est.at[it, pl.ds(dp, cp), pl.ds(dr, cr), :],
            send_sem=h_send.at[it, n], recv_sem=h_recv.at[it, n],
            device_id=(v + dv, t + dt), device_id_type=MESH_ID,
        )

    def region(n):
        dt, dv = DIRECTIONS[n]
        sp, dp, cp = {0: (rf, rf, nx), 1: (rf + nx, rf, rf), -1: (0, nx, rf)}[dt]
        sr, dr, cr = {0: (PAD, PAD, ny), 1: (PAD + ny, PAD, PAD), -1: (0, ny, PAD)}[dv]
        return sp, dp, cp, sr, dr, cr

    def overhang(it, n):
        dt, dv = DIRECTIONS[n]
        sp, dp, cp, sr, dr, cr = region(n)
        return pltpu.make_async_remote_copy(
            src_ref=ext.at[it, pl.ds(sp, cp), pl.ds(sr, cr), :],
            dst_ref=over.at[it, n, pl.ds(0, cp), pl.ds(0, cr), :],
            send_sem=o_send.at[it, n], recv_sem=o_recv.at[it, n],
            device_id=(v + dv, t + dt), device_id_type=MESH_ID,
        )

    def each(make, it, method, sending):
        for n, (dt, dv) in enumerate(DIRECTIONS):
            sign = 1 if sending else -1

            @pl.when(inside(sign * dt, sign * dv))
            def _(n=n):
                getattr(make(it, n), method)()

    def send_pack(d):
        peer = lax.rem(v + d, views)
        return pltpu.make_async_remote_copy(
            src_ref=pack.at[v], dst_ref=pack.at[v],
            send_sem=pk_send.at[d], recv_sem=pk_recv.at[views - d],
            device_id=(peer, t), device_id_type=MESH_ID,
        )

    def send_img(d):
        peer = lax.rem(v + d, views)
        return pltpu.make_async_remote_copy(
            src_ref=img_ref.at[0, :, pl.ds(pl.multiple_of(peer * ny, 8), ny), :],
            dst_ref=img.at[v],
            send_sem=img_send.at[d], recv_sem=img_recv.at[views - d],
            device_id=(peer, t), device_id_type=MESH_ID,
        )

    def arrived(buffer, sem, s, w):
        peer = lax.rem(v + s, views)
        pltpu.make_async_remote_copy(
            src_ref=buffer.at[w], dst_ref=buffer.at[w],
            send_sem=sem.at[s], recv_sem=sem.at[s],
            device_id=(peer, t), device_id_type=MESH_ID,
        ).wait_recv()

    each(halo, 0, "start", True)
    for d in range(1, views):
        send_pack(d).start()
    for d in range(1, views):
        send_img(d).start()

    rplane[...] = jnp.zeros(rplane.shape, f32)

    for it in range(ITERS):
        each(halo, it, "wait_recv", False)
        hi, lo = split(est[it].reshape(full * frame, nz))
        left[:, 0:nz] = hi
        left[:, nz : 2 * nz] = lo
        left[:, 2 * nz : 3 * nz] = hi

        def view(s, carry):
            w = lax.rem(v + s, views)
            if it == 0:
                @pl.when(s > 0)
                def _():
                    arrived(pack, pk_recv, s, w)

                row = jnp.broadcast_to(pack[w, nf + ns : nf + ns + 1, :], (nz, nz))
                i = lax.broadcasted_iota(jnp.int32, (nz, nz), 0)
                j = lax.broadcasted_iota(jnp.int32, (nz, nz), 1)
                matrix = pltpu.roll(row, nz - ra, axis=1, stride=1, stride_axis=0)
                matrix = jnp.where(jnp.abs(i - j) <= ra, matrix, 0.0)
                for ref, m in ((wconv, matrix), (wcorr, matrix.T)):
                    hi, lo = split(m)
                    ref[w, 0:nz, :] = hi
                    ref[w, nz : 2 * nz, :] = hi
                    ref[w, 2 * nz : 3 * nz, :] = lo

            planes[...] = jnp.dot(
                left[...], wconv[w], preferred_element_type=f32
            ).reshape(full, frame, nz)
            first = [pack[w, k : k + 1, :] for k in range(nf)]
            second = [pack[w, nf + k : nf + k + 1, :] for k in range(ns)]
            if it == 0:
                @pl.when(s > 0)
                def _():
                    arrived(img, img_recv, s, w)

                @pl.when(s == 0)
                def _():
                    own.wait()

            for x in range(nx):
                bplane[x] = sum(first[k] * planes[x + nf - 1 - k] for k in range(nf))
                blurred = sum(
                    second[k] * bplane[x, pl.ds(PAD + rs - k, ny), :] for k in range(ns)
                )
                rplane[x, pl.ds(2 * PAD, ny), :] = img[w, x] / blurred
                gplanes[x] = sum(
                    second[k] * rplane[x, pl.ds(PAD - rs + k, frame), :] for k in range(ns)
                )
            for x in range(full):
                total = sum(
                    first[k] * gplanes[x + k - (nf - 1)]
                    for k in range(nf)
                    if 0 <= x + k - (nf - 1) < nx
                )
                hi, lo = split(total)
                rows = pl.ds(x * frame, frame)
                left2[rows, 0:nz] = hi
                left2[rows, nz : 2 * nz] = lo
                left2[rows, 2 * nz : 3 * nz] = hi
            part = jnp.dot(left2[...], wcorr[w], preferred_element_type=f32).reshape(
                full, frame, nz
            )

            @pl.when(s == 0)
            def _():
                ext[it] = part

            @pl.when(s > 0)
            def _():
                ext[it] = ext[it] + part

            return carry

        lax.fori_loop(0, views, view, 0)
        each(overhang, it, "start", True)
        for n, (dt, dv) in enumerate(DIRECTIONS):
            @pl.when(inside(-dt, -dv))
            def _(n=n):
                overhang(it, n).wait_recv()
                _, dp, cp, _, dr, cr = region(n)
                place = (it, pl.ds(dp, cp), pl.ds(dr, cr), slice(None))
                ext[place] = ext[place] + over[it, n, pl.ds(0, cp), pl.ds(0, cr), :]

        for x in range(nx):
            new = est[it, rf + x, mid, :] * (ext[it, rf + x, mid, :] / views)
            if it + 1 < ITERS:
                est[it + 1, rf + x, mid, :] = new
            else:
                out_ref[x] = new
        if it + 1 < ITERS:
            each(halo, it + 1, "start", True)

    for it in range(ITERS):
        each(halo, it, "wait_send", True)
        each(overhang, it, "wait_send", True)
    for d in range(1, views):
        send_pack(d).wait_send()
        send_img(d).wait_send()


def local(views, tiles, estimate, images, taps_first, taps_second, taps_axial):
    nx, ny, nz = estimate.shape
    rf, rs, ra = [(taps.shape[1] - 1) // 2 for taps in (taps_first, taps_second, taps_axial)]
    frame = ny + 2 * PAD
    full = nx + 2 * rf
    f32, bf16 = jnp.float32, jnp.bfloat16
    vmem = pl.BlockSpec(memory_space=pltpu.VMEM)
    dma = pltpu.SemaphoreType.DMA
    directions = len(DIRECTIONS)
    rows = -(-(2 * rf + 2 * rs + 3) // 8) * 8
    return pl.pallas_call(
        functools.partial(kernel, views, tiles, rf, rs, ra),
        out_shape=jax.ShapeDtypeStruct(estimate.shape, f32),
        in_specs=[vmem, pl.BlockSpec(memory_space=pl.ANY), vmem, vmem, vmem],
        out_specs=vmem,
        scratch_shapes=[
            pltpu.VMEM((ITERS, full, frame, nz), f32),
            pltpu.VMEM((ITERS, full, frame, nz), f32),
            pltpu.VMEM((full, frame, nz), f32),
            pltpu.VMEM((nx, frame, nz), f32),
            pltpu.VMEM((nx, frame + 2 * PAD, nz), f32),
            pltpu.VMEM((nx, frame, nz), f32),
            pltpu.VMEM((full * frame, 3 * nz), bf16),
            pltpu.VMEM((full * frame, 3 * nz), bf16),
            pltpu.VMEM((views, 3 * nz, nz), bf16),
            pltpu.VMEM((views, 3 * nz, nz), bf16),
            pltpu.VMEM((views, rows, nz), f32),
            pltpu.VMEM((views, nx, ny, nz), f32),
            pltpu.VMEM((ITERS, directions, nx, ny, nz), f32),
            dma((views,)), dma((views,)), dma((views,)), dma((views,)), dma,
            dma((ITERS, directions)), dma((ITERS, directions)),
            dma((ITERS, directions)), dma((ITERS, directions)),
        ],
        compiler_params=pltpu.CompilerParams(
            collective_id=0, has_side_effects=True, vmem_limit_bytes=40 * 2**20
        ),
    )(estimate, images, taps_first, taps_second, taps_axial)


def solution(mesh):
    in_specs = (
        P("tile", "view", None),
        P("view", "tile", None, None),
        P("view", None),
        P("view", None),
        P("view", None),
    )
    out_specs = P("tile", "view", None)
    call = functools.partial(local, mesh.shape["view"], mesh.shape["tile"])
    return jax.shard_map(call, mesh=mesh, in_specs=in_specs, out_specs=out_specs, check_vma=False)
```

```python
import functools

import jax
import jax.numpy as jnp
from jax import lax
from jax.experimental import pallas as pl
from jax.experimental.pallas import tpu as pltpu
from jax.sharding import PartitionSpec as P

ITERS = 2
PAD = 8
DIRECTIONS = [(0, -1), (0, 1), (-1, -1), (-1, 1), (1, -1), (1, 1), (-1, 0), (1, 0)]
MESH_ID = pl.DeviceIdType.MESH


def split(x):
    hi = x.astype(jnp.bfloat16)
    lo = (x - hi.astype(jnp.float32)).astype(jnp.bfloat16)
    return hi, lo


def kernel(
    views, tiles, rf, rs, ra,
    est_hbm, img_ref, tf_hbm, ts_hbm, ta_hbm, out_ref,
    tf_ref, ts_ref, ta_ref, est, ext, planes, bplane, rplane, gplanes, left, left2, wconv, wcorr, pack, img, inverse, over, wide,
    img_send, img_recv, pk_send, pk_recv, local_sem, in_sem, h_send, h_recv, o_send, o_recv,
):
    nx, ny, nz = est_hbm.shape
    nf, ns, na = 2 * rf + 1, 2 * rs + 1, 2 * ra + 1
    frame = ny + 2 * PAD
    full = nx + 2 * rf
    v = lax.axis_index("view")
    t = lax.axis_index("tile")
    mid = pl.ds(PAD, ny)
    f32 = jnp.float32

    def inside(dt, dv):
        ok = None
        for d, at, count in ((dt, t, tiles), (dv, v, views)):
            if d:
                here = at + d < count if d > 0 else at + d >= 0
                ok = here if ok is None else jnp.logical_and(ok, here)
        return ok

    own = pltpu.make_async_copy(
        img_ref.at[0, :, pl.ds(pl.multiple_of(v * ny, 8), ny), :], img.at[v], local_sem
    )
    own.start()

    moves = [
        pltpu.make_async_copy(source, target, in_sem.at[n])
        for n, (source, target) in enumerate(
            ((tf_hbm, tf_ref), (ts_hbm, ts_ref), (ta_hbm, ta_ref))
        )
    ]
    for move in moves:
        move.start()
    est[0] = jnp.zeros(est.shape[1:], f32)

    barrier = pltpu.get_barrier_semaphore()
    for d in range(1, views):
        peer = lax.rem(v + d, views)
        pl.semaphore_signal(barrier, inc=1, device_id=(peer, t), device_id_type=MESH_ID)
    for dt, dv in DIRECTIONS:
        if dt:
            @pl.when(inside(dt, dv))
            def _(dt=dt, dv=dv):
                pl.semaphore_signal(
                    barrier, inc=1, device_id=(v + dv, t + dt), device_id_type=MESH_ID
                )

    start = pltpu.make_async_copy(est_hbm, est.at[0, pl.ds(rf, nx), mid, :], in_sem.at[3])
    start.start()
    pack[v] = jnp.zeros(pack.shape[1:], f32)
    rplane[...] = jnp.zeros(rplane.shape, f32)
    for move in moves:
        move.wait()
    for k in range(nf):
        pack[v, k : k + 1, :] = jnp.broadcast_to(tf_ref[0:1, k : k + 1], (1, nz))
    for k in range(ns):
        pack[v, nf + k : nf + k + 1, :] = jnp.broadcast_to(ts_ref[0:1, k : k + 1], (1, nz))
    pack[v, nf + ns : nf + ns + 1, 0:na] = ta_ref[...]
    start.wait()

    sides = jnp.where(t > 0, 1, 0) + jnp.where(t < tiles - 1, 1, 0)
    rows = 1 + jnp.where(v > 0, 1, 0) + jnp.where(v < views - 1, 1, 0)
    pl.semaphore_wait(barrier, views - 1 + sides * rows)

    def halo(n):
        dt, dv = DIRECTIONS[n]
        sp, dp, cp = {0: (rf, rf, nx), 1: (nx, 0, rf), -1: (rf, rf + nx, rf)}[dt]
        sr, dr, cr = {0: (PAD, PAD, ny), 1: (ny, 0, PAD), -1: (PAD, PAD + ny, PAD)}[dv]
        return pltpu.make_async_remote_copy(
            src_ref=est.at[0, pl.ds(sp, cp), pl.ds(sr, cr), :],
            dst_ref=est.at[0, pl.ds(dp, cp), pl.ds(dr, cr), :],
            send_sem=h_send.at[n], recv_sem=h_recv.at[n],
            device_id=(v + dv, t + dt), device_id_type=MESH_ID,
        )

    def region(it, n):
        dt, dv = DIRECTIONS[n]
        if it + 1 < ITERS:
            sp, dp, cp = {
                0: (0, 0, full), 1: (full - 2 * rf, 0, 2 * rf), -1: (0, full - 2 * rf, 2 * rf)
            }[dt]
            sr, dr, cr = {
                0: (0, 0, frame), 1: (ny, 0, 2 * PAD), -1: (0, ny, 2 * PAD)
            }[dv]
        else:
            sp, dp, cp = {0: (rf, rf, nx), 1: (rf + nx, rf, rf), -1: (0, nx, rf)}[dt]
            sr, dr, cr = {0: (PAD, PAD, ny), 1: (PAD + ny, PAD, PAD), -1: (0, ny, PAD)}[dv]
        return sp, dp, cp, sr, dr, cr

    def landing(it, n):
        return wide.at[it, n] if it + 1 < ITERS else over.at[n]

    def overhang(it, n):
        dt, dv = DIRECTIONS[n]
        sp, dp, cp, sr, dr, cr = region(it, n)
        return pltpu.make_async_remote_copy(
            src_ref=ext.at[it, pl.ds(sp, cp), pl.ds(sr, cr), :],
            dst_ref=landing(it, n).at[pl.ds(0, cp), pl.ds(0, cr), :],
            send_sem=o_send.at[it, n], recv_sem=o_recv.at[it, n],
            device_id=(v + dv, t + dt), device_id_type=MESH_ID,
        )

    def each(make, method, sending):
        for n, (dt, dv) in enumerate(DIRECTIONS):
            sign = 1 if sending else -1

            @pl.when(inside(sign * dt, sign * dv))
            def _(n=n):
                getattr(make(n), method)()

    def send_pack(d):
        peer = lax.rem(v + d, views)
        return pltpu.make_async_remote_copy(
            src_ref=pack.at[v], dst_ref=pack.at[v],
            send_sem=pk_send.at[d], recv_sem=pk_recv.at[views - d],
            device_id=(peer, t), device_id_type=MESH_ID,
        )

    def send_img(d):
        peer = lax.rem(v + d, views)
        return pltpu.make_async_remote_copy(
            src_ref=img_ref.at[0, :, pl.ds(pl.multiple_of(peer * ny, 8), ny), :],
            dst_ref=img.at[v],
            send_sem=img_send.at[d], recv_sem=img_recv.at[views - d],
            device_id=(peer, t), device_id_type=MESH_ID,
        )

    def arrived(buffer, sem, s, w):
        peer = lax.rem(v + s, views)
        pltpu.make_async_remote_copy(
            src_ref=buffer.at[w], dst_ref=buffer.at[w],
            send_sem=sem.at[s], recv_sem=sem.at[s],
            device_id=(peer, t), device_id_type=MESH_ID,
        ).wait_recv()

    for d in range(1, views):
        send_pack(d).start()
    each(halo, "start", True)
    for d in range(1, views):
        send_img(d).start()

    def prepare(s, w):
        @pl.when(s > 0)
        def _():
            arrived(pack, pk_recv, s, w)

        row = jnp.broadcast_to(pack[w, nf + ns : nf + ns + 1, :], (nz, nz))
        i = lax.broadcasted_iota(jnp.int32, (nz, nz), 0)
        j = lax.broadcasted_iota(jnp.int32, (nz, nz), 1)
        matrix = pltpu.roll(row, nz - ra, axis=1, stride=1, stride_axis=0)
        matrix = jnp.where(jnp.abs(i - j) <= ra, matrix, 0.0)
        for ref, m in ((wconv, matrix), (wcorr, matrix.T)):
            hi, lo = split(m)
            ref[w, 0:nz, :] = hi
            ref[w, nz : 2 * nz, :] = hi
            ref[w, 2 * nz : 3 * nz, :] = lo

    def taps(w):
        first = [pack[w, k : k + 1, :] for k in range(nf)]
        second = [pack[w, nf + k : nf + k + 1, :] for k in range(ns)]
        return first, second

    def spread(w):
        planes[...] = jnp.dot(left[...], wconv[w], preferred_element_type=f32).reshape(
            full, frame, nz
        )

    def blurred(x, first, second):
        bplane[x] = sum(first[k] * planes[x + nf - 1 - k] for k in range(nf))
        return sum(second[k] * bplane[x, pl.ds(PAD + rs - k, ny), :] for k in range(ns))

    def gather(x, ratio, second):
        rplane[x, pl.ds(2 * PAD, ny), :] = ratio
        gplanes[x] = sum(
            second[k] * rplane[x, pl.ds(PAD - rs + k, frame), :] for k in range(ns)
        )

    def finish(it, s, w, first):
        for x in range(full):
            total = sum(
                first[k] * gplanes[x + k - (nf - 1)]
                for k in range(nf)
                if 0 <= x + k - (nf - 1) < nx
            )
            hi, lo = split(total)
            rows = pl.ds(x * frame, frame)
            left2[rows, 0:nz] = hi
            left2[rows, nz : 2 * nz] = lo
            left2[rows, 2 * nz : 3 * nz] = hi
        part = jnp.dot(left2[...], wcorr[w], preferred_element_type=f32).reshape(
            full, frame, nz
        )

        @pl.when(s == 0)
        def _():
            ext[it] = part

        @pl.when(s > 0)
        def _():
            ext[it] = ext[it] + part

    def invert(s, carry):
        w = lax.rem(v + s, views)
        spread(w)
        first, second = taps(w)
        for x in range(nx):
            inverse[w, x] = 1.0 / blurred(x, first, second)
        return carry

    def correct(s, carry):
        w = lax.rem(v + s, views)

        @pl.when(s > 0)
        def _():
            arrived(img, img_recv, s, w)

        @pl.when(s == 0)
        def _():
            own.wait()

        first, second = taps(w)
        for x in range(nx):
            gather(x, img[w, x] * inverse[w, x], second)
        finish(0, s, w, first)
        return carry

    def both(it, s, carry):
        w = lax.rem(v + s, views)
        spread(w)
        first, second = taps(w)
        for x in range(nx):
            gather(x, img[w, x] / blurred(x, first, second), second)
        finish(it, s, w, first)
        return carry

    def weights(s, carry):
        prepare(s, lax.rem(v + s, views))
        return carry

    lax.fori_loop(0, views, weights, 0)
    each(halo, "wait_recv", False)
    for it in range(ITERS):
        hi, lo = split(est[it].reshape(full * frame, nz))
        left[:, 0:nz] = hi
        left[:, nz : 2 * nz] = lo
        left[:, 2 * nz : 3 * nz] = hi
        if it == 0:
            lax.fori_loop(0, views, invert, 0)
            lax.fori_loop(0, views, correct, 0)
        else:
            lax.fori_loop(0, views, functools.partial(both, it), 0)
        each(functools.partial(overhang, it), "start", True)
        last = it + 1 == ITERS
        if not last:
            est[it + 1] = ext[it]
        for n, (dt, dv) in enumerate(DIRECTIONS):
            @pl.when(inside(-dt, -dv))
            def _(n=n, it=it, last=last):
                overhang(it, n).wait_recv()
                _, dp, cp, _, dr, cr = region(it, n)
                to = ext.at[it] if last else est.at[it + 1]
                place = (pl.ds(dp, cp), pl.ds(dr, cr), slice(None))
                to[place] = to[place] + landing(it, n)[pl.ds(0, cp), pl.ds(0, cr), :]

        if last:
            for x in range(nx):
                out_ref[x] = est[it, rf + x, mid, :] * (ext[it, rf + x, mid, :] / views)
        else:
            est[it + 1] = est[it] * (est[it + 1] / views)

    each(halo, "wait_send", True)
    for it in range(ITERS):
        each(functools.partial(overhang, it), "wait_send", True)
    for d in range(1, views):
        send_pack(d).wait_send()
        send_img(d).wait_send()


def local(views, tiles, estimate, images, taps_first, taps_second, taps_axial):
    nx, ny, nz = estimate.shape
    rf, rs, ra = [(taps.shape[1] - 1) // 2 for taps in (taps_first, taps_second, taps_axial)]
    frame = ny + 2 * PAD
    full = nx + 2 * rf
    f32, bf16 = jnp.float32, jnp.bfloat16
    vmem = pl.BlockSpec(memory_space=pltpu.VMEM)
    dma = pltpu.SemaphoreType.DMA
    directions = len(DIRECTIONS)
    rows = -(-(2 * rf + 2 * rs + 3) // 8) * 8
    return pl.pallas_call(
        functools.partial(kernel, views, tiles, rf, rs, ra),
        out_shape=jax.ShapeDtypeStruct(estimate.shape, f32),
        in_specs=[pl.BlockSpec(memory_space=pltpu.HBM)] * 5,
        out_specs=vmem,
        scratch_shapes=[
            pltpu.VMEM(taps_first.shape, f32),
            pltpu.VMEM(taps_second.shape, f32),
            pltpu.VMEM(taps_axial.shape, f32),
            pltpu.VMEM((ITERS, full, frame, nz), f32),
            pltpu.VMEM((ITERS, full, frame, nz), f32),
            pltpu.VMEM((full, frame, nz), f32),
            pltpu.VMEM((nx, frame, nz), f32),
            pltpu.VMEM((nx, frame + 2 * PAD, nz), f32),
            pltpu.VMEM((nx, frame, nz), f32),
            pltpu.VMEM((full * frame, 3 * nz), bf16),
            pltpu.VMEM((full * frame, 3 * nz), bf16),
            pltpu.VMEM((views, 3 * nz, nz), bf16),
            pltpu.VMEM((views, 3 * nz, nz), bf16),
            pltpu.VMEM((views, rows, nz), f32),
            pltpu.VMEM((views, nx, ny, nz), f32),
            pltpu.VMEM((views, nx, ny, nz), f32),
            pltpu.VMEM((directions, nx, ny, nz), f32),
            pltpu.VMEM((ITERS - 1, directions, full, frame, nz), f32),
            dma((views,)), dma((views,)), dma((views,)), dma((views,)), dma, dma((4,)),
            dma((directions,)), dma((directions,)),
            dma((ITERS, directions)), dma((ITERS, directions)),
        ],
        compiler_params=pltpu.CompilerParams(
            collective_id=0, has_side_effects=True, vmem_limit_bytes=60 * 2**20
        ),
    )(estimate, images, taps_first, taps_second, taps_axial)


def solution(mesh):
    in_specs = (
        P("tile", "view", None),
        P("view", "tile", None, None),
        P("view", None),
        P("view", None),
        P("view", None),
    )
    out_specs = P("tile", "view", None)
    call = functools.partial(local, mesh.shape["view"], mesh.shape["tile"])
    return jax.shard_map(call, mesh=mesh, in_specs=in_specs, out_specs=out_specs, check_vma=False)
```

```python
import functools

import jax
import jax.numpy as jnp
from jax import lax
from jax.experimental import pallas as pl
from jax.experimental.pallas import tpu as pltpu
from jax.sharding import PartitionSpec as P

ITERS = 2
PAD = 8
DIRECTIONS = [(0, -1), (0, 1), (-1, -1), (-1, 1), (1, -1), (1, 1), (-1, 0), (1, 0)]
MESH_ID = pl.DeviceIdType.MESH


def split(x):
    hi = x.astype(jnp.bfloat16)
    lo = (x - hi.astype(jnp.float32)).astype(jnp.bfloat16)
    return hi, lo


def kernel(
    views, tiles, rf, rs, ra,
    est_hbm, img_ref, tf_hbm, ts_hbm, ta_hbm, out_ref,
    tf_ref, ts_ref, ta_ref, est, ext, planes, bplane, rplane, gplanes, left, left2, wconv, wcorr, pack, img, inverse, over, wide,
    img_send, img_recv, pk_send, pk_recv, local_sem, in_sem, h_send, h_recv, o_send, o_recv,
):
    nx, ny, nz = est_hbm.shape
    nf, ns, na = 2 * rf + 1, 2 * rs + 1, 2 * ra + 1
    frame = ny + 2 * PAD
    full = nx + 2 * rf
    v = lax.axis_index("view")
    t = lax.axis_index("tile")
    mid = pl.ds(PAD, ny)
    f32 = jnp.float32

    def inside(dt, dv):
        ok = None
        for d, at, count in ((dt, t, tiles), (dv, v, views)):
            if d:
                here = at + d < count if d > 0 else at + d >= 0
                ok = here if ok is None else jnp.logical_and(ok, here)
        return ok

    own = pltpu.make_async_copy(
        img_ref.at[0, :, pl.ds(pl.multiple_of(v * ny, 8), ny), :], img.at[v], local_sem
    )
    own.start()

    moves = [
        pltpu.make_async_copy(source, target, in_sem.at[n])
        for n, (source, target) in enumerate(
            ((tf_hbm, tf_ref), (ts_hbm, ts_ref), (ta_hbm, ta_ref))
        )
    ]
    for move in moves:
        move.start()
    est[0] = jnp.zeros(est.shape[1:], f32)

    barrier = pltpu.get_barrier_semaphore()
    for d in range(1, views):
        peer = lax.rem(v + d, views)
        pl.semaphore_signal(barrier, inc=1, device_id=(peer, t), device_id_type=MESH_ID)
    for dt, dv in DIRECTIONS:
        if dt:
            @pl.when(inside(dt, dv))
            def _(dt=dt, dv=dv):
                pl.semaphore_signal(
                    barrier, inc=1, device_id=(v + dv, t + dt), device_id_type=MESH_ID
                )

    start = pltpu.make_async_copy(est_hbm, est.at[0, pl.ds(rf, nx), mid, :], in_sem.at[3])
    start.start()
    pack[v] = jnp.zeros(pack.shape[1:], f32)
    rplane[...] = jnp.zeros(rplane.shape, f32)
    for move in moves:
        move.wait()
    for k in range(nf):
        pack[v, k : k + 1, :] = jnp.broadcast_to(tf_ref[0:1, k : k + 1], (1, nz))
    for k in range(ns):
        pack[v, nf + k : nf + k + 1, :] = jnp.broadcast_to(ts_ref[0:1, k : k + 1], (1, nz))
    pack[v, nf + ns : nf + ns + 1, 0:na] = ta_ref[...]
    start.wait()

    sides = jnp.where(t > 0, 1, 0) + jnp.where(t < tiles - 1, 1, 0)
    rows = 1 + jnp.where(v > 0, 1, 0) + jnp.where(v < views - 1, 1, 0)
    pl.semaphore_wait(barrier, views - 1 + sides * rows)

    def halo(n):
        dt, dv = DIRECTIONS[n]
        sp, dp, cp = {0: (rf, rf, nx), 1: (nx, 0, rf), -1: (rf, rf + nx, rf)}[dt]
        sr, dr, cr = {0: (PAD, PAD, ny), 1: (ny, 0, PAD), -1: (PAD, PAD + ny, PAD)}[dv]
        return pltpu.make_async_remote_copy(
            src_ref=est.at[0, pl.ds(sp, cp), pl.ds(sr, cr), :],
            dst_ref=est.at[0, pl.ds(dp, cp), pl.ds(dr, cr), :],
            send_sem=h_send.at[n], recv_sem=h_recv.at[n],
            device_id=(v + dv, t + dt), device_id_type=MESH_ID,
        )

    def region(it, n):
        dt, dv = DIRECTIONS[n]
        if it + 1 < ITERS:
            sp, dp, cp = {
                0: (0, 0, full), 1: (full - 2 * rf, 0, 2 * rf), -1: (0, full - 2 * rf, 2 * rf)
            }[dt]
            sr, dr, cr = {
                0: (0, 0, frame), 1: (ny, 0, 2 * PAD), -1: (0, ny, 2 * PAD)
            }[dv]
        else:
            sp, dp, cp = {0: (rf, rf, nx), 1: (rf + nx, rf, rf), -1: (0, nx, rf)}[dt]
            sr, dr, cr = {0: (PAD, PAD, ny), 1: (PAD + ny, PAD, PAD), -1: (0, ny, PAD)}[dv]
        return sp, dp, cp, sr, dr, cr

    def landing(it, n):
        return wide.at[it, n] if it + 1 < ITERS else over.at[n]

    def overhang(it, n):
        dt, dv = DIRECTIONS[n]
        sp, dp, cp, sr, dr, cr = region(it, n)
        return pltpu.make_async_remote_copy(
            src_ref=ext.at[it, pl.ds(sp, cp), pl.ds(sr, cr), :],
            dst_ref=landing(it, n).at[pl.ds(0, cp), pl.ds(0, cr), :],
            send_sem=o_send.at[it, n], recv_sem=o_recv.at[it, n],
            device_id=(v + dv, t + dt), device_id_type=MESH_ID,
        )

    def each(make, method, sending):
        for n, (dt, dv) in enumerate(DIRECTIONS):
            sign = 1 if sending else -1

            @pl.when(inside(sign * dt, sign * dv))
            def _(n=n):
                getattr(make(n), method)()

    def send_pack(d):
        peer = lax.rem(v + d, views)
        return pltpu.make_async_remote_copy(
            src_ref=pack.at[v], dst_ref=pack.at[v],
            send_sem=pk_send.at[d], recv_sem=pk_recv.at[views - d],
            device_id=(peer, t), device_id_type=MESH_ID,
        )

    def send_img(d):
        peer = lax.rem(v + d, views)
        return pltpu.make_async_remote_copy(
            src_ref=img_ref.at[0, :, pl.ds(pl.multiple_of(peer * ny, 8), ny), :],
            dst_ref=img.at[v],
            send_sem=img_send.at[d], recv_sem=img_recv.at[views - d],
            device_id=(peer, t), device_id_type=MESH_ID,
        )

    def arrived(buffer, sem, s, w):
        peer = lax.rem(v + s, views)
        pltpu.make_async_remote_copy(
            src_ref=buffer.at[w], dst_ref=buffer.at[w],
            send_sem=sem.at[s], recv_sem=sem.at[s],
            device_id=(peer, t), device_id_type=MESH_ID,
        ).wait_recv()

    for d in reversed(range(1, views)):
        send_pack(d).start()
    each(halo, "start", True)
    for d in reversed(range(1, views)):
        send_img(d).start()

    def prepare(s, w):
        @pl.when(s > 0)
        def _():
            arrived(pack, pk_recv, s, w)

        row = jnp.broadcast_to(pack[w, nf + ns : nf + ns + 1, :], (nz, nz))
        i = lax.broadcasted_iota(jnp.int32, (nz, nz), 0)
        j = lax.broadcasted_iota(jnp.int32, (nz, nz), 1)
        matrix = pltpu.roll(row, nz - ra, axis=1, stride=1, stride_axis=0)
        matrix = jnp.where(jnp.abs(i - j) <= ra, matrix, 0.0)
        for ref, m in ((wconv, matrix), (wcorr, matrix.T)):
            hi, lo = split(m)
            ref[w, 0:nz, :] = hi
            ref[w, nz : 2 * nz, :] = hi
            ref[w, 2 * nz : 3 * nz, :] = lo

    def taps(w):
        first = [pack[w, k : k + 1, :] for k in range(nf)]
        second = [pack[w, nf + k : nf + k + 1, :] for k in range(ns)]
        return first, second

    def spread(w):
        planes[...] = jnp.dot(left[...], wconv[w], preferred_element_type=f32).reshape(
            full, frame, nz
        )

    def blurred(x, first, second):
        bplane[x] = sum(first[k] * planes[x + nf - 1 - k] for k in range(nf))
        return sum(second[k] * bplane[x, pl.ds(PAD + rs - k, ny), :] for k in range(ns))

    def gather(x, ratio, second):
        rplane[x, pl.ds(2 * PAD, ny), :] = ratio
        gplanes[x] = sum(
            second[k] * rplane[x, pl.ds(PAD - rs + k, frame), :] for k in range(ns)
        )

    def finish(it, s, w, first):
        for x in range(full):
            total = sum(
                first[k] * gplanes[x + k - (nf - 1)]
                for k in range(nf)
                if 0 <= x + k - (nf - 1) < nx
            )
            hi, lo = split(total)
            rows = pl.ds(x * frame, frame)
            left2[rows, 0:nz] = hi
            left2[rows, nz : 2 * nz] = lo
            left2[rows, 2 * nz : 3 * nz] = hi
        part = jnp.dot(left2[...], wcorr[w], preferred_element_type=f32).reshape(
            full, frame, nz
        )

        @pl.when(s == 0)
        def _():
            ext[it] = part

        @pl.when(s > 0)
        def _():
            ext[it] = ext[it] + part

    def invert(s, carry):
        w = lax.rem(v + s, views)
        spread(w)
        first, second = taps(w)
        for x in range(nx):
            inverse[w, x] = 1.0 / blurred(x, first, second)
        return carry

    def correct(s, carry):
        w = lax.rem(v + s, views)

        @pl.when(s > 0)
        def _():
            arrived(img, img_recv, s, w)

        @pl.when(s == 0)
        def _():
            own.wait()

        first, second = taps(w)
        for x in range(nx):
            gather(x, img[w, x] * inverse[w, x], second)
        finish(0, s, w, first)
        return carry

    def both(it, s, carry):
        w = lax.rem(v + s, views)
        spread(w)
        first, second = taps(w)
        for x in range(nx):
            gather(x, img[w, x] / blurred(x, first, second), second)
        finish(it, s, w, first)
        return carry

    def weights(s, carry):
        prepare(s, lax.rem(v + s, views))
        return carry

    lax.fori_loop(0, views, weights, 0)
    each(halo, "wait_recv", False)
    for it in range(ITERS):
        hi, lo = split(est[it].reshape(full * frame, nz))
        left[:, 0:nz] = hi
        left[:, nz : 2 * nz] = lo
        left[:, 2 * nz : 3 * nz] = hi
        if it == 0:
            lax.fori_loop(0, views, invert, 0)
            lax.fori_loop(0, views, correct, 0)
        else:
            lax.fori_loop(0, views, functools.partial(both, it), 0)
        each(functools.partial(overhang, it), "start", True)
        last = it + 1 == ITERS
        if not last:
            est[it + 1] = ext[it]
        for n, (dt, dv) in enumerate(DIRECTIONS):
            @pl.when(inside(-dt, -dv))
            def _(n=n, it=it, last=last):
                overhang(it, n).wait_recv()
                _, dp, cp, _, dr, cr = region(it, n)
                to = ext.at[it] if last else est.at[it + 1]
                place = (pl.ds(dp, cp), pl.ds(dr, cr), slice(None))
                to[place] = to[place] + landing(it, n)[pl.ds(0, cp), pl.ds(0, cr), :]

        if last:
            for x in range(nx):
                out_ref[x] = est[it, rf + x, mid, :] * (ext[it, rf + x, mid, :] / views)
        else:
            est[it + 1] = est[it] * (est[it + 1] / views)

    each(halo, "wait_send", True)
    for it in range(ITERS):
        each(functools.partial(overhang, it), "wait_send", True)
    for d in range(1, views):
        send_pack(d).wait_send()
        send_img(d).wait_send()


def local(views, tiles, estimate, images, taps_first, taps_second, taps_axial):
    nx, ny, nz = estimate.shape
    rf, rs, ra = [(taps.shape[1] - 1) // 2 for taps in (taps_first, taps_second, taps_axial)]
    frame = ny + 2 * PAD
    full = nx + 2 * rf
    f32, bf16 = jnp.float32, jnp.bfloat16
    vmem = pl.BlockSpec(memory_space=pltpu.VMEM)
    dma = pltpu.SemaphoreType.DMA
    directions = len(DIRECTIONS)
    rows = -(-(2 * rf + 2 * rs + 3) // 8) * 8
    return pl.pallas_call(
        functools.partial(kernel, views, tiles, rf, rs, ra),
        out_shape=jax.ShapeDtypeStruct(estimate.shape, f32),
        in_specs=[pl.BlockSpec(memory_space=pltpu.HBM)] * 5,
        out_specs=vmem,
        scratch_shapes=[
            pltpu.VMEM(taps_first.shape, f32),
            pltpu.VMEM(taps_second.shape, f32),
            pltpu.VMEM(taps_axial.shape, f32),
            pltpu.VMEM((ITERS, full, frame, nz), f32),
            pltpu.VMEM((ITERS, full, frame, nz), f32),
            pltpu.VMEM((full, frame, nz), f32),
            pltpu.VMEM((nx, frame, nz), f32),
            pltpu.VMEM((nx, frame + 2 * PAD, nz), f32),
            pltpu.VMEM((nx, frame, nz), f32),
            pltpu.VMEM((full * frame, 3 * nz), bf16),
            pltpu.VMEM((full * frame, 3 * nz), bf16),
            pltpu.VMEM((views, 3 * nz, nz), bf16),
            pltpu.VMEM((views, 3 * nz, nz), bf16),
            pltpu.VMEM((views, rows, nz), f32),
            pltpu.VMEM((views, nx, ny, nz), f32),
            pltpu.VMEM((views, nx, ny, nz), f32),
            pltpu.VMEM((directions, nx, ny, nz), f32),
            pltpu.VMEM((ITERS - 1, directions, full, frame, nz), f32),
            dma((views,)), dma((views,)), dma((views,)), dma((views,)), dma, dma((4,)),
            dma((directions,)), dma((directions,)),
            dma((ITERS, directions)), dma((ITERS, directions)),
        ],
        compiler_params=pltpu.CompilerParams(
            collective_id=0, has_side_effects=True, vmem_limit_bytes=60 * 2**20
        ),
    )(estimate, images, taps_first, taps_second, taps_axial)


def solution(mesh):
    in_specs = (
        P("tile", "view", None),
        P("view", "tile", None, None),
        P("view", None),
        P("view", None),
        P("view", None),
    )
    out_specs = P("tile", "view", None)
    call = functools.partial(local, mesh.shape["view"], mesh.shape["tile"])
    return jax.shard_map(call, mesh=mesh, in_specs=in_specs, out_specs=out_specs, check_vma=False)
```

```python
import functools

import jax
import jax.numpy as jnp
from jax import lax
from jax.experimental import pallas as pl
from jax.experimental.pallas import tpu as pltpu
from jax.sharding import PartitionSpec as P

ITERS = 2
PAD = 8
DIRECTIONS = [(0, -1), (0, 1), (-1, -1), (-1, 1), (1, -1), (1, 1), (-1, 0), (1, 0)]
MESH_ID = pl.DeviceIdType.MESH


def split(x):
    hi = x.astype(jnp.bfloat16)
    lo = (x - hi.astype(jnp.float32)).astype(jnp.bfloat16)
    return hi, lo


def kernel(
    views, tiles, rf, rs, ra,
    est_hbm, img_ref, tf_hbm, ts_hbm, ta_hbm, out_ref,
    tf_ref, ts_ref, ta_ref, est, ext, planes, bplane, rplane, gplanes, left, left2, wconv, wcorr, pack, img, inverse, over, wide,
    img_send, img_recv, pk_send, pk_recv, local_sem, in_sem, h_send, h_recv, o_send, o_recv,
):
    nx, ny, nz = est_hbm.shape
    nf, ns, na = 2 * rf + 1, 2 * rs + 1, 2 * ra + 1
    frame = ny + 2 * PAD
    full = nx + 2 * rf
    v = lax.axis_index("view")
    t = lax.axis_index("tile")
    mid = pl.ds(PAD, ny)
    f32 = jnp.float32

    def inside(dt, dv):
        ok = None
        for d, at, count in ((dt, t, tiles), (dv, v, views)):
            if d:
                here = at + d < count if d > 0 else at + d >= 0
                ok = here if ok is None else jnp.logical_and(ok, here)
        return ok

    own = pltpu.make_async_copy(
        img_ref.at[0, :, pl.ds(pl.multiple_of(v * ny, 8), ny), :], img.at[v], local_sem
    )
    own.start()

    moves = [
        pltpu.make_async_copy(source, target, in_sem.at[n])
        for n, (source, target) in enumerate(
            ((tf_hbm, tf_ref), (ts_hbm, ts_ref), (ta_hbm, ta_ref))
        )
    ]
    for move in moves:
        move.start()
    est[0] = jnp.zeros(est.shape[1:], f32)

    barrier = pltpu.get_barrier_semaphore()
    for d in range(1, views):
        peer = lax.rem(v + d, views)
        pl.semaphore_signal(barrier, inc=1, device_id=(peer, t), device_id_type=MESH_ID)
    for dt, dv in DIRECTIONS:
        if dt:
            @pl.when(inside(dt, dv))
            def _(dt=dt, dv=dv):
                pl.semaphore_signal(
                    barrier, inc=1, device_id=(v + dv, t + dt), device_id_type=MESH_ID
                )

    start = pltpu.make_async_copy(est_hbm, est.at[0, pl.ds(rf, nx), mid, :], in_sem.at[3])
    start.start()
    pack[v] = jnp.zeros(pack.shape[1:], f32)
    rplane[...] = jnp.zeros(rplane.shape, f32)
    for move in moves:
        move.wait()
    for k in range(nf):
        pack[v, k : k + 1, :] = jnp.broadcast_to(tf_ref[0:1, k : k + 1], (1, nz))
    for k in range(ns):
        pack[v, nf + k : nf + k + 1, :] = jnp.broadcast_to(ts_ref[0:1, k : k + 1], (1, nz))
    pack[v, nf + ns : nf + ns + 1, 0:na] = ta_ref[...]
    start.wait()

    def prepare(s, w):
        @pl.when(s > 0)
        def _():
            arrived(pack, pk_recv, s, w)

        row = jnp.broadcast_to(pack[w, nf + ns : nf + ns + 1, :], (nz, nz))
        i = lax.broadcasted_iota(jnp.int32, (nz, nz), 0)
        j = lax.broadcasted_iota(jnp.int32, (nz, nz), 1)
        matrix = pltpu.roll(row, nz - ra, axis=1, stride=1, stride_axis=0)
        matrix = jnp.where(jnp.abs(i - j) <= ra, matrix, 0.0)
        for ref, m in ((wconv, matrix), (wcorr, matrix.T)):
            hi, lo = split(m)
            ref[w, 0:nz, :] = hi
            ref[w, nz : 2 * nz, :] = hi
            ref[w, 2 * nz : 3 * nz, :] = lo

    prepare(0, v)

    sides = jnp.where(t > 0, 1, 0) + jnp.where(t < tiles - 1, 1, 0)
    rows = 1 + jnp.where(v > 0, 1, 0) + jnp.where(v < views - 1, 1, 0)
    pl.semaphore_wait(barrier, views - 1 + sides * rows)

    def halo(n):
        dt, dv = DIRECTIONS[n]
        sp, dp, cp = {0: (rf, rf, nx), 1: (nx, 0, rf), -1: (rf, rf + nx, rf)}[dt]
        sr, dr, cr = {0: (PAD, PAD, ny), 1: (ny, 0, PAD), -1: (PAD, PAD + ny, PAD)}[dv]
        return pltpu.make_async_remote_copy(
            src_ref=est.at[0, pl.ds(sp, cp), pl.ds(sr, cr), :],
            dst_ref=est.at[0, pl.ds(dp, cp), pl.ds(dr, cr), :],
            send_sem=h_send.at[n], recv_sem=h_recv.at[n],
            device_id=(v + dv, t + dt), device_id_type=MESH_ID,
        )

    def region(it, n):
        dt, dv = DIRECTIONS[n]
        if it + 1 < ITERS:
            sp, dp, cp = {
                0: (0, 0, full), 1: (full - 2 * rf, 0, 2 * rf), -1: (0, full - 2 * rf, 2 * rf)
            }[dt]
            sr, dr, cr = {
                0: (0, 0, frame), 1: (ny, 0, 2 * PAD), -1: (0, ny, 2 * PAD)
            }[dv]
        else:
            sp, dp, cp = {0: (rf, rf, nx), 1: (rf + nx, rf, rf), -1: (0, nx, rf)}[dt]
            sr, dr, cr = {0: (PAD, PAD, ny), 1: (PAD + ny, PAD, PAD), -1: (0, ny, PAD)}[dv]
        return sp, dp, cp, sr, dr, cr

    def landing(it, n):
        return wide.at[it, n] if it + 1 < ITERS else over.at[n]

    def overhang(it, n):
        dt, dv = DIRECTIONS[n]
        sp, dp, cp, sr, dr, cr = region(it, n)
        return pltpu.make_async_remote_copy(
            src_ref=ext.at[it, pl.ds(sp, cp), pl.ds(sr, cr), :],
            dst_ref=landing(it, n).at[pl.ds(0, cp), pl.ds(0, cr), :],
            send_sem=o_send.at[it, n], recv_sem=o_recv.at[it, n],
            device_id=(v + dv, t + dt), device_id_type=MESH_ID,
        )

    def each(make, method, sending, chosen=range(len(DIRECTIONS))):
        for n in chosen:
            dt, dv = DIRECTIONS[n]
            sign = 1 if sending else -1

            @pl.when(inside(sign * dt, sign * dv))
            def _(n=n):
                getattr(make(n), method)()

    def send_pack(d):
        peer = lax.rem(v + d, views)
        return pltpu.make_async_remote_copy(
            src_ref=pack.at[v], dst_ref=pack.at[v],
            send_sem=pk_send.at[d], recv_sem=pk_recv.at[views - d],
            device_id=(peer, t), device_id_type=MESH_ID,
        )

    def send_img(d):
        peer = lax.rem(v + d, views)
        return pltpu.make_async_remote_copy(
            src_ref=img_ref.at[0, :, pl.ds(pl.multiple_of(peer * ny, 8), ny), :],
            dst_ref=img.at[v],
            send_sem=img_send.at[d], recv_sem=img_recv.at[views - d],
            device_id=(peer, t), device_id_type=MESH_ID,
        )

    def arrived(buffer, sem, s, w):
        peer = lax.rem(v + s, views)
        pltpu.make_async_remote_copy(
            src_ref=buffer.at[w], dst_ref=buffer.at[w],
            send_sem=sem.at[s], recv_sem=sem.at[s],
            device_id=(peer, t), device_id_type=MESH_ID,
        ).wait_recv()

    for d in reversed(range(1, views)):
        send_pack(d).start()
    each(halo, "start", True, range(6))
    for d in reversed(range(1, views)):
        send_img(d).start()
    each(halo, "start", True, range(6, 8))

    def taps(w):
        first = [pack[w, k : k + 1, :] for k in range(nf)]
        second = [pack[w, nf + k : nf + k + 1, :] for k in range(ns)]
        return first, second

    def spread(w):
        planes[...] = jnp.dot(left[...], wconv[w], preferred_element_type=f32).reshape(
            full, frame, nz
        )

    def blurred(x, first, second):
        bplane[x] = sum(first[k] * planes[x + nf - 1 - k] for k in range(nf))
        return sum(second[k] * bplane[x, pl.ds(PAD + rs - k, ny), :] for k in range(ns))

    def gather(x, ratio, second):
        rplane[x, pl.ds(2 * PAD, ny), :] = ratio
        gplanes[x] = sum(
            second[k] * rplane[x, pl.ds(PAD - rs + k, frame), :] for k in range(ns)
        )

    def finish(it, s, w, first):
        for x in range(full):
            total = sum(
                first[k] * gplanes[x + k - (nf - 1)]
                for k in range(nf)
                if 0 <= x + k - (nf - 1) < nx
            )
            hi, lo = split(total)
            rows = pl.ds(x * frame, frame)
            left2[rows, 0:nz] = hi
            left2[rows, nz : 2 * nz] = lo
            left2[rows, 2 * nz : 3 * nz] = hi
        part = jnp.dot(left2[...], wcorr[w], preferred_element_type=f32).reshape(
            full, frame, nz
        )

        @pl.when(s == 0)
        def _():
            ext[it] = part

        @pl.when(s > 0)
        def _():
            ext[it] = ext[it] + part

    def invert(s, carry):
        w = lax.rem(v + s, views)
        spread(w)
        first, second = taps(w)
        for x in range(nx):
            inverse[w, x] = 1.0 / blurred(x, first, second)
        return carry

    def correct(s, carry):
        w = lax.rem(v + s, views)

        @pl.when(s > 0)
        def _():
            arrived(img, img_recv, s, w)

        @pl.when(s == 0)
        def _():
            own.wait()

        first, second = taps(w)
        for x in range(nx):
            gather(x, img[w, x] * inverse[w, x], second)
        finish(0, s, w, first)
        return carry

    def both(it, s, carry):
        w = lax.rem(v + s, views)
        spread(w)
        first, second = taps(w)
        for x in range(nx):
            gather(x, img[w, x] / blurred(x, first, second), second)
        finish(it, s, w, first)
        return carry

    def weights(s, carry):
        prepare(s, lax.rem(v + s, views))
        return carry

    lax.fori_loop(1, views, weights, 0)
    each(halo, "wait_recv", False)
    for it in range(ITERS):
        hi, lo = split(est[it].reshape(full * frame, nz))
        left[:, 0:nz] = hi
        left[:, nz : 2 * nz] = lo
        left[:, 2 * nz : 3 * nz] = hi
        if it == 0:
            lax.fori_loop(0, views, invert, 0)
            lax.fori_loop(0, views, correct, 0)
        else:
            lax.fori_loop(0, views, functools.partial(both, it), 0)
        each(functools.partial(overhang, it), "start", True)
        last = it + 1 == ITERS
        if not last:
            est[it + 1] = ext[it]
        for n, (dt, dv) in enumerate(DIRECTIONS):
            @pl.when(inside(-dt, -dv))
            def _(n=n, it=it, last=last):
                overhang(it, n).wait_recv()
                _, dp, cp, _, dr, cr = region(it, n)
                to = ext.at[it] if last else est.at[it + 1]
                place = (pl.ds(dp, cp), pl.ds(dr, cr), slice(None))
                to[place] = to[place] + landing(it, n)[pl.ds(0, cp), pl.ds(0, cr), :]

        if last:
            for x in range(nx):
                out_ref[x] = est[it, rf + x, mid, :] * (ext[it, rf + x, mid, :] / views)
        else:
            est[it + 1] = est[it] * (est[it + 1] / views)

    each(halo, "wait_send", True)
    for it in range(ITERS):
        each(functools.partial(overhang, it), "wait_send", True)
    for d in range(1, views):
        send_pack(d).wait_send()
        send_img(d).wait_send()


def local(views, tiles, estimate, images, taps_first, taps_second, taps_axial):
    nx, ny, nz = estimate.shape
    rf, rs, ra = [(taps.shape[1] - 1) // 2 for taps in (taps_first, taps_second, taps_axial)]
    frame = ny + 2 * PAD
    full = nx + 2 * rf
    f32, bf16 = jnp.float32, jnp.bfloat16
    vmem = pl.BlockSpec(memory_space=pltpu.VMEM)
    dma = pltpu.SemaphoreType.DMA
    directions = len(DIRECTIONS)
    rows = -(-(2 * rf + 2 * rs + 3) // 8) * 8
    return pl.pallas_call(
        functools.partial(kernel, views, tiles, rf, rs, ra),
        out_shape=jax.ShapeDtypeStruct(estimate.shape, f32),
        in_specs=[pl.BlockSpec(memory_space=pltpu.HBM)] * 5,
        out_specs=vmem,
        scratch_shapes=[
            pltpu.VMEM(taps_first.shape, f32),
            pltpu.VMEM(taps_second.shape, f32),
            pltpu.VMEM(taps_axial.shape, f32),
            pltpu.VMEM((ITERS, full, frame, nz), f32),
            pltpu.VMEM((ITERS, full, frame, nz), f32),
            pltpu.VMEM((full, frame, nz), f32),
            pltpu.VMEM((nx, frame, nz), f32),
            pltpu.VMEM((nx, frame + 2 * PAD, nz), f32),
            pltpu.VMEM((nx, frame, nz), f32),
            pltpu.VMEM((full * frame, 3 * nz), bf16),
            pltpu.VMEM((full * frame, 3 * nz), bf16),
            pltpu.VMEM((views, 3 * nz, nz), bf16),
            pltpu.VMEM((views, 3 * nz, nz), bf16),
            pltpu.VMEM((views, rows, nz), f32),
            pltpu.VMEM((views, nx, ny, nz), f32),
            pltpu.VMEM((views, nx, ny, nz), f32),
            pltpu.VMEM((directions, nx, ny, nz), f32),
            pltpu.VMEM((ITERS - 1, directions, full, frame, nz), f32),
            dma((views,)), dma((views,)), dma((views,)), dma((views,)), dma, dma((4,)),
            dma((directions,)), dma((directions,)),
            dma((ITERS, directions)), dma((ITERS, directions)),
        ],
        compiler_params=pltpu.CompilerParams(
            collective_id=0, has_side_effects=True, vmem_limit_bytes=60 * 2**20
        ),
    )(estimate, images, taps_first, taps_second, taps_axial)


def solution(mesh):
    in_specs = (
        P("tile", "view", None),
        P("view", "tile", None, None),
        P("view", None),
        P("view", None),
        P("view", None),
    )
    out_specs = P("tile", "view", None)
    call = functools.partial(local, mesh.shape["view"], mesh.shape["tile"])
    return jax.shard_map(call, mesh=mesh, in_specs=in_specs, out_specs=out_specs, check_vma=False)
```
